32 devices in a mesh: seq: 32 (over z, y, x, core).
Axes of the slice: x: 2, y: 2, z: 4, core: 2. Of those that a mesh axis runs over, the one named last changes fastest.
Arguments:
- features: float32 [16384, 512], P('seq'), may hold values from -6 to 6
- preacts: float32 [3, 16384, 512], P(None, 'seq'), may hold values from -6 to 6
- teacher: float32 [3, 16384, 512], P(None, 'seq'), may hold values from -6 to 6
- cotangent: float32 [16384, 512], P('seq'), may hold values from -6 to 6
- kernels: float32 [3, 3, 512, 512], replicated, may hold values from -0.15625 to 0.15625
Outputs:
- input_grad: float32 [16384, 512], P('seq')
- kernel_grad: float32 [3, 3, 512, 512], P(None, None, 'seq')
The draws below stay inside these ranges and needn't reach their ends.
All inputs are finite; a program needn't handle non-finite values.
Results may differ from the reference program's by a relative error of at most 0.0001.
Values sent between devices are 32-bit elements; how exact they have to be, the bound alone decides.
No kernel may reach another device: no remote copies, remote signals or barrier semaphores. Data moves between devices by JAX's collectives and lax.ppermute only.
A program may use at most 128 MiB of HBM per device.

```python
import math
import jax
import jax.numpy as jnp
from jax import lax

C = 512
BASE_SPACING = 512
LAYERS = 3
TAPS = 3
BINS = 16384


def spiked(array, own_key, source, target, shards_of, factor):
    owner, partner = [(jnp.arange(array.shape[dim]) // (array.shape[dim] // shards_of)).reshape([-1 if axis == dim else 1 for axis in range(array.ndim)]) for dim in (source, target)]
    chosen = jax.random.permutation(own_key, shards_of)[partner]
    strong = (owner == chosen) | (owner == (partner + shards_of // 2) % shards_of)
    return jnp.where(strong, factor * array, array)


def steps_of(key, shape, cuts, least, high):
    def one(axis_at, shards_of):
        draws = jax.random.uniform(jax.random.fold_in(jax.random.fold_in(key, 6), axis_at), (shards_of,), jnp.float32, least / len(cuts), high / len(cuts))
        return jnp.repeat(jnp.exp(draws), shape[axis_at] // shards_of).reshape((-1,) + (1,) * (len(shape) - axis_at - 1))

    factor_of = one(*cuts[0])
    for cut in cuts[1:]:
        factor_of = factor_of * one(*cut)
    return factor_of


def bell_draw(rng, extent, spread, reach, pieces=(), kind=jnp.bfloat16):
    loudness = steps_of(rng, extent, pieces, -0.22, 0.18) if pieces else 1.0
    array = jax.random.normal(rng, extent, jnp.float32) * spread * loudness
    return jnp.minimum(jnp.maximum(array, -reach), reach).astype(kind)


def heavy_noise(key, dims, spread, limit, shards, heavy, kind=jnp.bfloat16):
    values = spread * jax.random.normal(key, dims, jnp.float32)
    if shards:
        values = values * steps_of(key, dims, shards, -0.22, 0.18)
    return jnp.clip(spiked(values, jax.random.fold_in(key, 3), *heavy), -limit, limit).astype(kind)


def setup_inputs(seed: int = 0) -> dict:
    key_of = jax.random.split(jax.random.key(seed), 6)
    features = heavy_noise(key_of[0], (BINS, C), 1.0, 6.0, ((0, 32),), (0, 1, 32, 2.75), jnp.float32)
    preacts = bell_draw(key_of[1], (LAYERS, BINS, C), 1.0, 6.0, ((1, 32),), jnp.float32)
    teacher = bell_draw(key_of[2], (LAYERS, BINS, C), 1.0, 6.0, ((1, 32),), jnp.float32)
    cotangent = bell_draw(key_of[3], (BINS, C), 1.0, 6.0, ((0, 32),), jnp.float32)
    kernels = bell_draw(key_of[4], (LAYERS, TAPS, C, C), (3 * C) ** -0.5, 0.15625, (), jnp.float32)
    return {"features": features, "preacts": preacts, "teacher": teacher, "cotangent": cotangent, "kernels": kernels}


mimic_weight = 0.5

def gelu_response(linear_response):
    cdf = 0.5 * (1.0 + jax.scipy.special.erf(linear_response / math.sqrt(2.0)))
    return linear_response * cdf

def gelu_slope(linear_response):
    cdf = 0.5 * (1.0 + jax.scipy.special.erf(linear_response / math.sqrt(2.0)))
    density = jnp.exp(-0.5 * linear_response * linear_response) / math.sqrt(2.0 * math.pi)
    return cdf + linear_response * density

def matmul(left, right):
    return jnp.dot(left, right, precision=lax.Precision.HIGHEST, preferred_element_type=jnp.float32)

def inner(left, right):
    return lax.dot_general(left, right, (((0,), (0,)), ((), ())), precision=lax.Precision.HIGHEST, preferred_element_type=jnp.float32)

def reference(features, preacts, teacher, cotangent, kernels):
    states = [features]
    state = features
    for layer_number in range(LAYERS):
        state = state + gelu_response(preacts[layer_number])
        states.append(state)
    scale = 1.0 / math.sqrt(BINS)
    grad = cotangent
    layer_gradient_list = [None] * LAYERS
    for layer_number in range(LAYERS - 1, -1, -1):
        receptive_span = BASE_SPACING * 2 ** layer_number
        grad = grad + mimic_weight * (states[layer_number + 1] - teacher[layer_number])
        pre_grad = grad * gelu_slope(preacts[layer_number])
        zeros = jnp.zeros((receptive_span, pre_grad.shape[1]), pre_grad.dtype)
        grad_next = jnp.concatenate([pre_grad[receptive_span:], zeros], axis=0)
        grad_prev = jnp.concatenate([zeros, pre_grad[:-receptive_span]], axis=0)
        weights = kernels[layer_number]
        grad = grad + matmul(grad_next, weights[0].T) + matmul(pre_grad, weights[1].T) + matmul(grad_prev, weights[2].T)
        source = states[layer_number]
        layer_gradient_list[layer_number] = jnp.stack([inner(source, grad_next), inner(source, pre_grad), inner(source, grad_prev)]) * scale
    return (grad, jnp.stack(layer_gradient_list))
```

```python
import math

import jax
import jax.numpy as jnp
from jax import lax
from jax.experimental import pallas as pl
from jax.experimental.pallas import tpu as pltpu
from jax.sharding import PartitionSpec as P

BASE_SPACING = 512
LAYERS = 3
MIMIC_WEIGHT = 0.5
F32 = jnp.float32
STRIP = 32
PIECES = (2,)
GROUPS = (((0,), (1, 3), (2, 4)), ((0,), (2,), (4,), (3,), (1,)), ((0,), (2,), (4,), (3,), (1,)))
FIRST_SIXTEENTHS = 8
UNIT = 5 * 10**9
ORDER = (
    ("top", 0), ("prep", 0), ("turn", 0), ("w2", 0), ("ca2", 0), ("aa2", 0),
    ("w1", 0), ("cb2", 0), ("ca1", 0), ("m2", 0), ("ab2", 0), ("t2", 0), ("aa1", 0),
    ("w0", 0), ("cb1", 0), ("ca0", 0), ("m1", 0), ("ab1", 4), ("r2", 0), ("aa0", 0),
    ("t1", 0), ("m0", 0), ("cb0", 0),
    ("ab0", 0), ("t0", 0), ("r1", 0), ("r2", 0), ("r0", 0), ("r2", 0), ("r1", 0),
    ("r0", 0), ("r1", 0), ("r2", 0), ("r1", 0),
)


def paired(array, jump, parity):
    devices = lax.axis_size("seq")
    pairs = []
    for i in range(devices):
        j = i + jump if (i // jump) % 2 == parity else i - jump
        if 0 <= j < devices:
            pairs.append((i, j))
    return lax.ppermute(array, "seq", pairs)


def swapped(array, mask):
    devices = lax.axis_size("seq")
    return lax.ppermute(array, "seq", [(i, i ^ mask) for i in range(devices)])


def gelu_and_slope(u):
    cdf = 0.5 * (1.0 + lax.erf(u * math.sqrt(0.5)))
    density = jnp.exp(-0.5 * u * u) * (1.0 / math.sqrt(2.0 * math.pi))
    return u * cdf, cdf + u * density


def dot(left, right, precision=lax.Precision.HIGH):
    return jnp.dot(left, right, precision=precision, preferred_element_type=F32)


def dot_nt(left, right, precision=lax.Precision.HIGH):
    return lax.dot_general(
        left, right, (((1,), (1,)), ((), ())), precision=precision, preferred_element_type=F32
    )


class Line:
    def __init__(self, scalars):
        self.last = None
        self.scalars = scalars

    def __call__(self, body, inputs, outputs, limit=24, work=0):
        arrays, specs = [], []
        for item in inputs:
            array, spec = item if isinstance(item, tuple) else (item, None)
            arrays.append(array)
            specs.append(spec or pl.BlockSpec(array.shape, lambda i, s, n=array.ndim: (0,) * n))
        count = len(arrays)
        if self.last is not None:
            arrays.append(self.last)
            specs.append(pl.BlockSpec(memory_space=pl.ANY))
        total = len(arrays)

        def kernel(scalars, *refs):
            body(scalars, *refs[:count], *refs[total:])

        out = pl.pallas_call(
            kernel,
            grid_spec=pltpu.PrefetchScalarGridSpec(
                num_scalar_prefetch=1,
                grid=(1,),
                in_specs=specs,
                out_specs=[pl.BlockSpec(s, lambda i, _, n=len(s): (0,) * n) for s in outputs],
            ),
            out_shape=[jax.ShapeDtypeStruct(s, F32) for s in outputs],
            compiler_params=pltpu.CompilerParams(vmem_limit_bytes=limit * 2**20),
            cost_estimate=pl.CostEstimate(flops=work * UNIT, bytes_accessed=1024, transcendentals=0),
        )(self.scalars, *arrays)
        self.last = out[0]
        return out


class Scatter:
    def __init__(self, line, groups):
        self.line, self.groups, self.keep, self.received = line, list(groups), [], []
        (self.first,) = self.groups.pop(0)

    def add(self, send, keep):
        self.keep.append(keep)
        self.received.append([(0, swapped(send, 1 << self.first))])

    def step(self, work):
        bits = self.groups.pop(0)
        parts = 1 << len(bits)
        keeps, received = self.keep, self.received
        rows = keeps[0].shape[0] // parts
        columns = sum(k.shape[1] for k in keeps)
        flat = [array for group in received for _, array in group]
        count = len(keeps)

        def body(_, *refs):
            got, outs = refs[count : count + len(flat)], refs[count + len(flat) :]
            for q, out_ref in enumerate(outs):
                r = slice(q * rows, (q + 1) * rows)
                at = n = 0
                for keep_ref, group in zip(refs[:count], received):
                    value = keep_ref[r, :]
                    for _ in group:
                        value = value + got[n][r, :]
                        n += 1
                    out_ref[:, at : at + keep_ref.shape[1]] = value
                    at += keep_ref.shape[1]

        keep, *sends = self.line(body, [*keeps, *flat], [(rows, columns)] * parts, work=work)
        group = []
        for q, send in enumerate(sends, 1):
            mask = sum(1 << bit for n, bit in enumerate(reversed(bits)) if (q >> n) & 1)
            group.append((q, swapped(send, mask)))
        self.keep, self.received = [keep], [group]

    def result(self):
        assert not self.groups
        return sum((array for _, array in self.received[0]), self.keep[0])


def shards(features, preacts, teacher, cotangent, kernels):
    bins, channels = features.shape
    devices = lax.axis_size("seq")
    width = devices.bit_length() - 1
    me = lax.axis_index("seq")
    scale = 1.0 / math.sqrt(bins * devices)
    jumps = [BASE_SPACING * 2**layer // bins for layer in range(LAYERS)]
    groups = []
    for layer in GROUPS:
        known = [g for g in (tuple(b for b in bits if b < width) for bits in layer) if g]
        listed = [b for g in known for b in g]
        groups.append(known + [(b,) for b in range(width) if b not in listed])
    parity = jnp.stack([(me // jump) % 2 for jump in jumps]).astype(jnp.int32)
    cut = FIRST_SIXTEENTHS * bins // 16
    spans = ((0, cut), (cut, bins))
    line = Line(parity)
    full = (bins, channels)
    square = (channels, channels)
    parts = [(stop - start, channels) for start, stop in spans]

    def rows_of(array, c, lead=None):
        start, stop = spans[c]
        if lead is None:
            block = (pl.Element(stop - start), pl.Element(channels))
            return array, pl.BlockSpec(block, lambda i, s: (start, 0))
        block = (pl.Squeezed(), pl.Element(stop - start), pl.Element(channels))
        return array, pl.BlockSpec(block, lambda i, s: (lead, start, 0))

    def halo(gu, layer):
        return paired(gu, jumps[layer], 0), paired(gu, jumps[layer], 1)

    def strips(rows):
        return pl.loop(0, rows // STRIP)

    def strip(i):
        return pl.ds(pl.multiple_of(i * STRIP, STRIP), STRIP)

    def top():
        def body(_, x_ref, u0_ref, u1_ref, u2_ref, t_ref, cot_ref, g_ref, gu_ref):
            @strips(cut)
            def _(i):
                r = strip(i)
                x = x_ref[r, :] + gelu_and_slope(u0_ref[r, :])[0]
                x = x + gelu_and_slope(u1_ref[r, :])[0]
                response, slope = gelu_and_slope(u2_ref[r, :])
                g = cot_ref[r, :] + MIMIC_WEIGHT * (x + response - t_ref[r, :])
                g_ref[r, :] = g
                gu_ref[r, :] = g * slope

        ins = [rows_of(features, 0), *(rows_of(preacts, 0, l) for l in range(LAYERS))]
        ins += [rows_of(teacher, 0, 2), rows_of(cotangent, 0)]
        return line(body, ins, [parts[0]] * 2, 63)

    def prepare():
        def body(_, x_ref, u_ref, t_ref, cot_ref, *refs):
            x1_ref, x2_ref, *pairs, g_ref, gu_ref = refs

            def both(i, c):
                r = strip(i + spans[c][0] // STRIP)
                low = strip(i)
                h0_ref, s0_ref, h1_ref, s1_ref = pairs[4 * c : 4 * c + 4]
                response, s0_ref[low, :] = gelu_and_slope(u_ref[0, r, :])
                x1 = x_ref[r, :] + response
                x1_ref[r, :] = x1
                h0_ref[low, :] = MIMIC_WEIGHT * (x1 - t_ref[0, r, :])
                response, s1_ref[low, :] = gelu_and_slope(u_ref[1, r, :])
                x2 = x1 + response
                x2_ref[r, :] = x2
                h1_ref[low, :] = MIMIC_WEIGHT * (x2 - t_ref[1, r, :])
                return r, low, x2

            @strips(cut)
            def _(i):
                both(i, 0)

            @strips(bins - cut)
            def _(i):
                r, low, x2 = both(i, 1)
                response, slope = gelu_and_slope(u_ref[2, r, :])
                g = cot_ref[r, :] + MIMIC_WEIGHT * (x2 + response - t_ref[2, r, :])
                g_ref[low, :] = g
                gu_ref[low, :] = g * slope

        ins = [features, preacts, teacher, cotangent]
        return line(body, ins, [full] * 2 + [parts[0]] * 4 + [parts[1]] * 6, 56)

    def weights(layer):
        def body(_, *refs):
            for source, target in zip(refs[:3], refs[3:]):
                target[...] = source[...]

        block = (pl.Squeezed(), pl.Squeezed(), channels, channels)
        ins = [
            (kernels, pl.BlockSpec(block, lambda i, s: (layer, 2 * s[layer], 0, 0))),
            (kernels, pl.BlockSpec(block, lambda i, s: (layer, 1, 0, 0))),
            (kernels, pl.BlockSpec(block, lambda i, s: (layer, 2 - 2 * s[layer], 0, 0))),
        ]
        return line(body, ins, [square] * 3)

    def turn(xs):
        block = channels // devices
        sources = []
        for layer in range(LAYERS):
            row = jnp.arange(channels, dtype=jnp.int32)
            index = row // block
            target = jnp.zeros_like(row)
            for place, bit in enumerate(b for g in groups[layer] for b in g):
                target = target | (((index >> (width - 1 - place)) & 1) << bit)
            sources.append((target ^ me) * block + row % block)
        sources = jnp.stack(sources)[:, :, None]

        def body(_, source_ref, *refs):
            lanes = lax.broadcasted_iota(jnp.int32, (channels, channels), 1)
            for l in range(LAYERS):
                pick = jnp.where(lanes == source_ref[l], 1.0, 0.0)
                refs[LAYERS + l][...] = dot_nt(pick, refs[l][...])

        return line(body, [sources, *xs], [(channels, bins)] * LAYERS)

    def center(g, gu, w, carried=None):
        carry = [] if carried is None else [carried]

        def body(_, g_ref, gu_ref, w_ref, *refs):
            refs[len(carry)][...] = g_ref[...] + dot_nt(gu_ref[...], w_ref[...])
            if carry:
                refs[2][...] = refs[0][...]

        return line(body, [g, gu, w, *carry], [g.shape] + [c.shape for c in carry])

    def advance(base, sides, wp, wq, pull=None, slope=None, work=0):
        def body(_, base_ref, p_ref, q_ref, wp_ref, wq_ref, *refs):
            g = base_ref[...] + dot_nt(p_ref[...], wp_ref[...])
            g = g + dot_nt(q_ref[...], wq_ref[...])
            if pull is None:
                refs[0][...] = g
            else:
                pull_ref, slope_ref, g_ref, gu_ref = refs
                g = g + pull_ref[...]
                g_ref[...] = g
                gu_ref[...] = g * slope_ref[...]

        ins = [base, *sides, wp, wq]
        if pull is None:
            return line(body, ins, [base.shape], work=work)
        return line(body, ins + [pull, slope], [base.shape] * 2, work=work)

    rows = channels // 2

    def middle(layer, x, gu_a, gu_b, work):
        def body(_, x_ref, a_ref, b_ref, *outs):
            both = jnp.concatenate([a_ref[...], b_ref[...]], axis=0)
            value = dot(x_ref[...], both)
            for n, out_ref in enumerate(outs):
                out_ref[...] = value[rows * n : rows * (n + 1), :]

        keep, send = line(body, [x, gu_a, gu_b], [(rows, channels)] * 2, work=work)
        sums[layer].add(send, keep)

    def terms(layer, x, sides_a, sides_b, work):
        def body(s_ref, x_ref, *refs):
            for k in range(2):
                column = s_ref[layer] if k == 0 else 1 - s_ref[layer]
                place = pl.ds(pl.multiple_of(column * channels, channels), channels)
                both = jnp.concatenate([refs[k][...], refs[2 + k][...]], axis=0)
                value = dot(x_ref[...], both)
                for n, out_ref in enumerate(refs[4:]):
                    out_ref[:, place] = value[rows * n : rows * (n + 1), :]

        shapes = [(rows, 2 * channels)] * 2
        keep, send = line(body, [x, *sides_a, *sides_b], shapes, work=work)
        sums[layer].add(send, keep)

    sums = [Scatter(line, groups[layer]) for layer in range(LAYERS)]
    w, base, g, gu, halos = {}, {}, {}, {}, {}
    pull, slope = {}, {}
    for name, work in ORDER:
        kind, layer = name[:-1], int(name[-1]) if name[-1].isdigit() else None
        if name == "top":
            g["a"], gu["a", 2] = top()
            halos["a", 2] = halo(gu["a", 2], 2)
        elif name == "prep":
            x1, x2, *pairs, g["b"], carried = prepare()
            for c, key in enumerate("ab"):
                h = pairs[4 * c : 4 * c + 4]
                pull[key, 1], slope[key, 1], pull[key, 2], slope[key, 2] = h
        elif name == "turn":
            xt = turn((features, x1, x2))
        elif kind == "w":
            w[layer] = weights(layer)
        elif name == "ca2":
            base["a"], gu["b", 2] = center(g["a"], gu["a", 2], w[2][1], carried)
            halos["b", 2] = halo(gu["b", 2], 2)
        elif kind in ("ca", "cb"):
            key = kind[1]
            (base[key],) = center(g[key], gu[key, layer], w[layer][1])
        elif kind in ("aa", "ab"):
            key = kind[1]
            args = base[key], halos[key, layer], w[layer][0], w[layer][2]
            if layer:
                g[key], gu[key, layer - 1] = advance(
                    *args, pull[key, layer], slope[key, layer], work=work
                )
                halos[key, layer - 1] = halo(gu[key, layer - 1], layer - 1)
            else:
                (g[key],) = advance(*args, work=work)
        elif kind == "m":
            middle(layer, xt[layer], gu["a", layer], gu["b", layer], work)
        elif kind == "t":
            terms(layer, xt[layer], halos["a", layer], halos["b", layer], work)
        else:
            sums[layer].step(work)
    for s in sums:
        while s.groups:
            s.step(0)
    done = [s.result() for s in sums]
    grads = jnp.stack(done) * scale
    grads = grads.reshape(LAYERS, channels // devices, 3, channels).transpose(0, 2, 1, 3)
    grads = jnp.stack([grads[:, 1], grads[:, 0], grads[:, 2]], axis=1)
    return jnp.concatenate([g["a"], g["b"]], axis=0), grads


def solution(mesh):
    in_specs = (P("seq", None), P(None, "seq", None), P(None, "seq", None), P("seq", None), P())
    out_specs = (P("seq", None), P(None, None, "seq", None))
    return jax.shard_map(shards, mesh=mesh, in_specs=in_specs, out_specs=out_specs, check_vma=False)
```

```python
import math

import jax
import jax.numpy as jnp
from jax import lax
from jax.experimental import pallas as pl
from jax.experimental.pallas import tpu as pltpu
from jax.sharding import PartitionSpec as P

BASE_SPACING = 512
LAYERS = 3
MIMIC_WEIGHT = 0.5
F32 = jnp.float32
STRIP = 32
PIECES = (2,)
GROUPS = (((0,), (1, 2), (3, 4)), ((0,), (2,), (1, 3), (4,)), ((0,), (3,), (2, 4), (1,)))
FIRST_SIXTEENTHS = 7
UNIT = 5 * 10**9
ORDER = (('top', 0), ('prep', 0), ('w', 6), ('ca2', 1), ('cb2', 6), ('turn', 2), ('aa2', 1), ('ca1', 4), ('ab2', 0), ('t2', 1), ('m2', 2), ('aa1', 3), ('ca0', 0), ('cb1', 0), ('r2', 0), ('ab1', 1), ('t1', 10), ('cb0', 1), ('r1', 3), ('t0', 6), ('ab0', 0), ('r2', 4), ('r1', 0), ('r0', 0), ('r0', 0), ('r2', 0), ('r1', 6), ('aa0', 1))


def paired(array, jump, parity):
    devices = lax.axis_size("seq")
    pairs = []
    for i in range(devices):
        j = i + jump if (i // jump) % 2 == parity else i - jump
        if 0 <= j < devices:
            pairs.append((i, j))
    return lax.ppermute(array, "seq", pairs)


def swapped(array, mask):
    devices = lax.axis_size("seq")
    return lax.ppermute(array, "seq", [(i, i ^ mask) for i in range(devices)])


def gelu_and_slope(u):
    cdf = 0.5 * (1.0 + lax.erf(u * math.sqrt(0.5)))
    density = jnp.exp(-0.5 * u * u) * (1.0 / math.sqrt(2.0 * math.pi))
    return u * cdf, cdf + u * density


def dot(left, right, precision=lax.Precision.HIGH):
    return jnp.dot(left, right, precision=precision, preferred_element_type=F32)


def dot_nt(left, right, precision=lax.Precision.HIGH):
    return lax.dot_general(
        left, right, (((1,), (1,)), ((), ())), precision=precision, preferred_element_type=F32
    )


class Line:
    def __init__(self, scalars):
        self.last = None
        self.scalars = scalars

    def __call__(self, body, inputs, outputs, limit=24, work=0):
        arrays, specs = [], []
        for item in inputs:
            array, spec = item if isinstance(item, tuple) else (item, None)
            arrays.append(array)
            specs.append(spec or pl.BlockSpec(array.shape, lambda i, s, n=array.ndim: (0,) * n))
        count = len(arrays)
        if self.last is not None:
            arrays.append(self.last)
            specs.append(pl.BlockSpec(memory_space=pl.ANY))
        total = len(arrays)

        def kernel(scalars, *refs):
            body(scalars, *refs[:count], *refs[total:])

        out = pl.pallas_call(
            kernel,
            grid_spec=pltpu.PrefetchScalarGridSpec(
                num_scalar_prefetch=1,
                grid=(1,),
                in_specs=specs,
                out_specs=[pl.BlockSpec(s, lambda i, _, n=len(s): (0,) * n) for s in outputs],
            ),
            out_shape=[jax.ShapeDtypeStruct(s, F32) for s in outputs],
            compiler_params=pltpu.CompilerParams(vmem_limit_bytes=limit * 2**20),
            cost_estimate=pl.CostEstimate(flops=work * UNIT, bytes_accessed=1024, transcendentals=0),
        )(self.scalars, *arrays)
        self.last = out[0]
        return out


class Scatter:
    def __init__(self, line, groups):
        self.line, self.groups, self.keep, self.received = line, list(groups), [], []
        (self.first,) = self.groups.pop(0)

    def add(self, send, keep):
        self.keep.append(keep)
        self.received.append([(0, swapped(send, 1 << self.first))])

    def step(self, work):
        bits = self.groups.pop(0)
        parts = 1 << len(bits)
        keeps, received = self.keep, self.received
        rows = keeps[0].shape[0] // parts
        columns = sum(k.shape[1] for k in keeps)
        flat = [array for group in received for _, array in group]
        count = len(keeps)

        def body(_, *refs):
            got, outs = refs[count : count + len(flat)], refs[count + len(flat) :]
            for q, out_ref in enumerate(outs):
                r = slice(q * rows, (q + 1) * rows)
                at = n = 0
                for keep_ref, group in zip(refs[:count], received):
                    value = keep_ref[r, :]
                    for _ in group:
                        value = value + got[n][r, :]
                        n += 1
                    out_ref[:, at : at + keep_ref.shape[1]] = value
                    at += keep_ref.shape[1]

        keep, *sends = self.line(body, [*keeps, *flat], [(rows, columns)] * parts, work=work)
        group = []
        for q, send in enumerate(sends, 1):
            mask = sum(1 << bit for n, bit in enumerate(reversed(bits)) if (q >> n) & 1)
            group.append((q, swapped(send, mask)))
        self.keep, self.received = [keep], [group]

    def result(self):
        assert not self.groups
        return sum((array for _, array in self.received[0]), self.keep[0])


def shards(features, preacts, teacher, cotangent, kernels):
    bins, channels = features.shape
    devices = lax.axis_size("seq")
    width = devices.bit_length() - 1
    me = lax.axis_index("seq")
    scale = 1.0 / math.sqrt(bins * devices)
    jumps = [BASE_SPACING * 2**layer // bins for layer in range(LAYERS)]
    groups = []
    for layer in GROUPS:
        known = [g for g in (tuple(b for b in bits if b < width) for bits in layer) if g]
        listed = [b for g in known for b in g]
        groups.append(known + [(b,) for b in range(width) if b not in listed])
    scalars = jnp.stack([*((me // jump) % 2 for jump in jumps), me]).astype(jnp.int32)
    cut = FIRST_SIXTEENTHS * bins // 16
    spans = ((0, cut), (cut, bins))
    line = Line(scalars)
    full = (bins, channels)
    square = (channels, channels)
    parts = [(stop - start, channels) for start, stop in spans]

    def rows_of(array, c, lead=None):
        start, stop = spans[c]
        if lead is None:
            block = (pl.Element(stop - start), pl.Element(channels))
            return array, pl.BlockSpec(block, lambda i, s: (start, 0))
        block = (pl.Squeezed(), pl.Element(stop - start), pl.Element(channels))
        return array, pl.BlockSpec(block, lambda i, s: (lead, start, 0))

    def halo(gu, layer):
        return paired(gu, jumps[layer], 0), paired(gu, jumps[layer], 1)

    def strips(rows):
        return pl.loop(0, rows // STRIP)

    def strip(i):
        return pl.ds(pl.multiple_of(i * STRIP, STRIP), STRIP)

    def top():
        def body(_, x_ref, u0_ref, u1_ref, u2_ref, t_ref, cot_ref, g_ref, gu_ref):
            @strips(cut)
            def _(i):
                r = strip(i)
                x = x_ref[r, :] + gelu_and_slope(u0_ref[r, :])[0]
                x = x + gelu_and_slope(u1_ref[r, :])[0]
                response, slope = gelu_and_slope(u2_ref[r, :])
                g = cot_ref[r, :] + MIMIC_WEIGHT * (x + response - t_ref[r, :])
                g_ref[r, :] = g
                gu_ref[r, :] = g * slope

        ins = [rows_of(features, 0), *(rows_of(preacts, 0, l) for l in range(LAYERS))]
        ins += [rows_of(teacher, 0, 2), rows_of(cotangent, 0)]
        return line(body, ins, [parts[0]] * 2, 63)

    def prepare():
        def body(_, x_ref, u_ref, t_ref, cot_ref, *refs):
            x1_ref, x2_ref, *pairs, g_ref, gu_ref = refs

            def both(i, c):
                r = strip(i + spans[c][0] // STRIP)
                low = strip(i)
                h0_ref, s0_ref, h1_ref, s1_ref = pairs[4 * c : 4 * c + 4]
                response, s0_ref[low, :] = gelu_and_slope(u_ref[0, r, :])
                x1 = x_ref[r, :] + response
                x1_ref[r, :] = x1
                h0_ref[low, :] = MIMIC_WEIGHT * (x1 - t_ref[0, r, :])
                response, s1_ref[low, :] = gelu_and_slope(u_ref[1, r, :])
                x2 = x1 + response
                x2_ref[r, :] = x2
                h1_ref[low, :] = MIMIC_WEIGHT * (x2 - t_ref[1, r, :])
                return r, low, x2

            @strips(cut)
            def _(i):
                both(i, 0)

            @strips(bins - cut)
            def _(i):
                r, low, x2 = both(i, 1)
                response, slope = gelu_and_slope(u_ref[2, r, :])
                g = cot_ref[r, :] + MIMIC_WEIGHT * (x2 + response - t_ref[2, r, :])
                g_ref[low, :] = g
                gu_ref[low, :] = g * slope

        ins = [features, preacts, teacher, cotangent]
        return line(body, ins, [full] * 2 + [parts[0]] * 4 + [parts[1]] * 6, 56)

    def weights():
        def body(scalars, k_ref, *targets):
            for layer in range(LAYERS):
                side = 2 * scalars[layer]
                for n, k in enumerate((side, 1, 2 - side)):
                    targets[3 * layer + n][...] = k_ref[layer, k]

        out = line(body, [kernels], [square] * (3 * LAYERS), 32)
        return [out[3 * layer : 3 * layer + 3] for layer in range(LAYERS)]

    def turn(xs):
        block = channels // devices
        uses = [(0, 0), (0, 1), (1, 1), (1, 2), (2, 2)]

        def body(scalars, *refs):
            row = lax.broadcasted_iota(jnp.int32, (channels, 1), 0)
            index = row // block
            lanes = lax.broadcasted_iota(jnp.int32, (channels, channels), 1)
            picks = []
            for layer in range(LAYERS):
                target = jnp.zeros_like(row)
                for place, bit in enumerate(b for g in groups[layer] for b in g):
                    target = target | (((index >> (width - 1 - place)) & 1) << bit)
                source = (target ^ scalars[LAYERS]) * block + row % block
                picks.append(jnp.where(lanes == source, 1.0, 0.0))
            for n, (x, order) in enumerate(uses):
                refs[LAYERS + n][...] = dot_nt(picks[order], refs[x][...])

        return dict(zip(uses, line(body, xs, [(channels, bins)] * len(uses))))

    def center(g, gu, w, carried=None):
        carry = [] if carried is None else [carried]

        def body(_, g_ref, gu_ref, w_ref, *refs):
            refs[len(carry)][...] = g_ref[...] + dot_nt(gu_ref[...], w_ref[...])
            if carry:
                refs[2][...] = refs[0][...]

        return line(body, [g, gu, w, *carry], [g.shape] + [c.shape for c in carry])

    def advance(base, sides, wp, wq, pull=None, slope=None, work=0):
        def body(_, base_ref, p_ref, q_ref, wp_ref, wq_ref, *refs):
            g = base_ref[...] + dot_nt(p_ref[...], wp_ref[...])
            g = g + dot_nt(q_ref[...], wq_ref[...])
            if pull is None:
                refs[0][...] = g
            else:
                pull_ref, slope_ref, g_ref, gu_ref = refs
                g = g + pull_ref[...]
                g_ref[...] = g
                gu_ref[...] = g * slope_ref[...]

        ins = [base, *sides, wp, wq]
        if pull is None:
            return line(body, ins, [base.shape], work=work)
        return line(body, ins + [pull, slope], [base.shape] * 2, work=work)

    rows = channels // 2

    def add(layer, x, body, inputs, taps, work):
        keep, send = line(body, [x, *inputs], [(rows, len(taps) * channels)] * 2, work=work)
        sums[layer].add(send, keep)
        columns[layer].extend(taps)

    def store(outs, place, value):
        for n, out_ref in enumerate(outs):
            out_ref[:, place] = value[rows * n : rows * (n + 1), :]

    def middle(layer, work):
        def body(_, x_ref, a_ref, b_ref, *outs):
            both = jnp.concatenate([a_ref[...], b_ref[...]], axis=0)
            store(outs, slice(0, channels), dot(x_ref[...], both))

        add(layer, xt[layer, layer], body, [gu["a", layer], gu["b", layer]], [(layer, 1)], work)

    def terms(layer, work):
        below = layer - 1
        ins = [*halos["a", layer], *halos["b", layer]]
        if layer:
            ins += [gu["a", below], gu["b", below], xt[below, layer]]

        def body(s_ref, x_ref, *refs):
            outs = refs[len(ins) :]
            for k in range(2):
                column = s_ref[layer] if k == 0 else 1 - s_ref[layer]
                place = pl.ds(pl.multiple_of(column * channels, channels), channels)
                both = jnp.concatenate([refs[k][...], refs[2 + k][...]], axis=0)
                store(outs, place, dot(x_ref[...], both))
            if layer:
                both = jnp.concatenate([refs[4][...], refs[5][...]], axis=0)
                store(outs, slice(2 * channels, 3 * channels), dot(refs[6][...], both))

        taps = [(layer, 0), (layer, 2)] + ([(below, 1)] if layer else [])
        add(layer, xt[layer, layer], body, ins, taps, work)

    sums = [Scatter(line, groups[layer]) for layer in range(LAYERS)]
    columns = [[] for _ in range(LAYERS)]
    w, base, g, gu, halos = {}, {}, {}, {}, {}
    pull, slope = {}, {}
    for name, work in ORDER:
        kind, layer = name[:-1], int(name[-1]) if name[-1].isdigit() else None
        if name == "top":
            g["a"], gu["a", 2] = top()
            halos["a", 2] = halo(gu["a", 2], 2)
        elif name == "prep":
            x1, x2, *pairs, g["b"], carried = prepare()
            gu["b", 2] = carried
            for c, key in enumerate("ab"):
                h = pairs[4 * c : 4 * c + 4]
                pull[key, 1], slope[key, 1], pull[key, 2], slope[key, 2] = h
        elif name == "turn":
            xt = turn((features, x1, x2))
        elif name == "w":
            w = weights()
        elif name == "ca2":
            base["a"], gu["b", 2] = center(g["a"], gu["a", 2], w[2][1], carried)
            halos["b", 2] = halo(gu["b", 2], 2)
        elif kind in ("ca", "cb"):
            key = kind[1]
            (base[key],) = center(g[key], gu[key, layer], w[layer][1])
        elif kind in ("aa", "ab"):
            key = kind[1]
            args = base[key], halos[key, layer], w[layer][0], w[layer][2]
            if layer:
                g[key], gu[key, layer - 1] = advance(
                    *args, pull[key, layer], slope[key, layer], work=work
                )
                halos[key, layer - 1] = halo(gu[key, layer - 1], layer - 1)
            else:
                (g[key],) = advance(*args, work=work)
        elif kind == "m":
            middle(layer, work)
        elif kind == "t":
            terms(layer, work)
        elif sums[layer].groups:
            sums[layer].step(work)
    for s in sums:
        while s.groups:
            s.step(0)
    done = [s.result() for s in sums]
    taps = {}
    for total, names in zip(done, columns):
        for n, tap in enumerate(names):
            taps[tap] = total[:, n * channels : (n + 1) * channels]
    grads = jnp.stack([jnp.stack([taps[layer, k] for k in range(3)]) for layer in range(LAYERS)])
    grads = grads * scale
    return jnp.concatenate([g["a"], g["b"]], axis=0), grads


def solution(mesh):
    in_specs = (P("seq", None), P(None, "seq", None), P(None, "seq", None), P("seq", None), P())
    out_specs = (P("seq", None), P(None, None, "seq", None))
    return jax.shard_map(shards, mesh=mesh, in_specs=in_specs, out_specs=out_specs, check_vma=False)
```

```python
import math

import jax
import jax.numpy as jnp
from jax import lax
from jax.experimental import pallas as pl
from jax.experimental.pallas import tpu as pltpu
from jax.sharding import PartitionSpec as P

BASE_SPACING = 512
LAYERS = 3
MIMIC_WEIGHT = 0.5
F32 = jnp.float32
STRIP = 32
PIECES = (2,)
GROUPS = (((0,), (1, 2), (3, 4)), ((0,), (1,), (3,), (4,), (2,)), ((0,), (3,), (2, 4), (1,)))
FIRST_SIXTEENTHS = 8
UNIT = 5 * 10**9
ORDER = (('top', 4), ('prep', 6), ('w', 1), ('ca2', 0), ('turn', 0), ('aa2', 4), ('ca1', 1), ('cb2', 0), ('ab2', 1), ('cb1', 3), ('m2', 4), ('t2', 4), ('aa1', 10), ('r2', 0), ('ab1', 2), ('t1', 0), ('r2', 3), ('r1', 10), ('ca0', 4), ('cb0', 6), ('aa0', 0), ('t0', 1), ('r1', 4), ('r2', 3), ('r0', 0), ('r1', 0), ('ab0', 0), ('r0', 6), ('r1', 0))


def paired(array, jump, parity):
    devices = lax.axis_size("seq")
    pairs = []
    for i in range(devices):
        j = i + jump if (i // jump) % 2 == parity else i - jump
        if 0 <= j < devices:
            pairs.append((i, j))
    return lax.ppermute(array, "seq", pairs)


def swapped(array, mask):
    devices = lax.axis_size("seq")
    return lax.ppermute(array, "seq", [(i, i ^ mask) for i in range(devices)])


def gelu_and_slope(u):
    cdf = 0.5 * (1.0 + lax.erf(u * math.sqrt(0.5)))
    density = jnp.exp(-0.5 * u * u) * (1.0 / math.sqrt(2.0 * math.pi))
    return u * cdf, cdf + u * density


def dot(left, right, precision=lax.Precision.HIGH):
    return jnp.dot(left, right, precision=precision, preferred_element_type=F32)


def dot_nt(left, right, precision=lax.Precision.HIGH):
    return lax.dot_general(
        left, right, (((1,), (1,)), ((), ())), precision=precision, preferred_element_type=F32
    )


class Line:
    def __init__(self, scalars):
        self.last = None
        self.scalars = scalars

    def __call__(self, body, inputs, outputs, limit=24, work=0):
        arrays, specs = [], []
        for item in inputs:
            array, spec = item if isinstance(item, tuple) else (item, None)
            arrays.append(array)
            specs.append(spec or pl.BlockSpec(array.shape, lambda i, s, n=array.ndim: (0,) * n))
        count = len(arrays)
        if self.last is not None:
            arrays.append(self.last)
            specs.append(pl.BlockSpec(memory_space=pl.ANY))
        total = len(arrays)

        def kernel(scalars, *refs):
            body(scalars, *refs[:count], *refs[total:])

        out = pl.pallas_call(
            kernel,
            grid_spec=pltpu.PrefetchScalarGridSpec(
                num_scalar_prefetch=1,
                grid=(1,),
                in_specs=specs,
                out_specs=[pl.BlockSpec(s, lambda i, _, n=len(s): (0,) * n) for s in outputs],
            ),
            out_shape=[jax.ShapeDtypeStruct(s, F32) for s in outputs],
            compiler_params=pltpu.CompilerParams(vmem_limit_bytes=limit * 2**20),
            cost_estimate=pl.CostEstimate(flops=work * UNIT, bytes_accessed=1024, transcendentals=0),
        )(self.scalars, *arrays)
        self.last = out[0]
        return out


class Scatter:
    def __init__(self, line, groups):
        self.line, self.groups, self.keep, self.received = line, list(groups), [], []
        (self.first,) = self.groups.pop(0)

    def add(self, send, keep):
        self.keep.append(keep)
        self.received.append([(0, swapped(send, 1 << self.first))])

    def step(self, work):
        bits = self.groups.pop(0)
        parts = 1 << len(bits)
        keeps, received = self.keep, self.received
        rows = keeps[0].shape[0] // parts
        columns = sum(k.shape[1] for k in keeps)
        flat = [array for group in received for _, array in group]
        count = len(keeps)

        def body(_, *refs):
            got, outs = refs[count : count + len(flat)], refs[count + len(flat) :]
            for q, out_ref in enumerate(outs):
                r = slice(q * rows, (q + 1) * rows)
                at = n = 0
                for keep_ref, group in zip(refs[:count], received):
                    value = keep_ref[r, :]
                    for _ in group:
                        value = value + got[n][r, :]
                        n += 1
                    out_ref[:, at : at + keep_ref.shape[1]] = value
                    at += keep_ref.shape[1]

        keep, *sends = self.line(body, [*keeps, *flat], [(rows, columns)] * parts, work=work)
        group = []
        for q, send in enumerate(sends, 1):
            mask = sum(1 << bit for n, bit in enumerate(reversed(bits)) if (q >> n) & 1)
            group.append((q, swapped(send, mask)))
        self.keep, self.received = [keep], [group]

    def result(self):
        assert not self.groups
        return sum((array for _, array in self.received[0]), self.keep[0])


def shards(features, preacts, teacher, cotangent, kernels):
    bins, channels = features.shape
    devices = lax.axis_size("seq")
    width = devices.bit_length() - 1
    me = lax.axis_index("seq")
    scale = 1.0 / math.sqrt(bins * devices)
    jumps = [BASE_SPACING * 2**layer // bins for layer in range(LAYERS)]
    groups = []
    for layer in GROUPS:
        known = [g for g in (tuple(b for b in bits if b < width) for bits in layer) if g]
        listed = [b for g in known for b in g]
        groups.append(known + [(b,) for b in range(width) if b not in listed])
    scalars = jnp.stack([*((me // jump) % 2 for jump in jumps), me]).astype(jnp.int32)
    cut = FIRST_SIXTEENTHS * bins // 16
    spans = ((0, cut), (cut, bins))
    line = Line(scalars)
    full = (bins, channels)
    square = (channels, channels)
    parts = [(stop - start, channels) for start, stop in spans]

    def rows_of(array, c, lead=None):
        start, stop = spans[c]
        if lead is None:
            block = (pl.Element(stop - start), pl.Element(channels))
            return array, pl.BlockSpec(block, lambda i, s: (start, 0))
        block = (pl.Squeezed(), pl.Element(stop - start), pl.Element(channels))
        return array, pl.BlockSpec(block, lambda i, s: (lead, start, 0))

    def halo(gu, layer):
        return paired(gu, jumps[layer], 0), paired(gu, jumps[layer], 1)

    def strips(rows):
        return pl.loop(0, rows // STRIP)

    def strip(i):
        return pl.ds(pl.multiple_of(i * STRIP, STRIP), STRIP)

    def top():
        def body(_, x_ref, u0_ref, u1_ref, u2_ref, t_ref, cot_ref, g_ref, gu_ref):
            @strips(cut)
            def _(i):
                r = strip(i)
                x = x_ref[r, :] + gelu_and_slope(u0_ref[r, :])[0]
                x = x + gelu_and_slope(u1_ref[r, :])[0]
                response, slope = gelu_and_slope(u2_ref[r, :])
                g = cot_ref[r, :] + MIMIC_WEIGHT * (x + response - t_ref[r, :])
                g_ref[r, :] = g
                gu_ref[r, :] = g * slope

        ins = [rows_of(features, 0), *(rows_of(preacts, 0, l) for l in range(LAYERS))]
        ins += [rows_of(teacher, 0, 2), rows_of(cotangent, 0)]
        return line(body, ins, [parts[0]] * 2, 63)

    def prepare():
        def body(_, x_ref, u_ref, t_ref, cot_ref, *refs):
            x1_ref, x2_ref, *pairs, g_ref, gu_ref = refs

            def both(i, c):
                r = strip(i + spans[c][0] // STRIP)
                low = strip(i)
                h0_ref, s0_ref, h1_ref, s1_ref = pairs[4 * c : 4 * c + 4]
                response, s0_ref[low, :] = gelu_and_slope(u_ref[0, r, :])
                x1 = x_ref[r, :] + response
                x1_ref[r, :] = x1
                h0_ref[low, :] = MIMIC_WEIGHT * (x1 - t_ref[0, r, :])
                response, s1_ref[low, :] = gelu_and_slope(u_ref[1, r, :])
                x2 = x1 + response
                x2_ref[r, :] = x2
                h1_ref[low, :] = MIMIC_WEIGHT * (x2 - t_ref[1, r, :])
                return r, low, x2

            @strips(cut)
            def _(i):
                both(i, 0)

            @strips(bins - cut)
            def _(i):
                r, low, x2 = both(i, 1)
                response, slope = gelu_and_slope(u_ref[2, r, :])
                g = cot_ref[r, :] + MIMIC_WEIGHT * (x2 + response - t_ref[2, r, :])
                g_ref[low, :] = g
                gu_ref[low, :] = g * slope

        ins = [features, preacts, teacher, cotangent]
        return line(body, ins, [full] * 2 + [parts[0]] * 4 + [parts[1]] * 6, 56)

    def weights():
        def body(scalars, k_ref, *targets):
            for layer in range(LAYERS):
                side = 2 * scalars[layer]
                for n, k in enumerate((side, 1, 2 - side)):
                    targets[3 * layer + n][...] = k_ref[layer, k]

        out = line(body, [kernels], [square] * (3 * LAYERS), 32)
        return [out[3 * layer : 3 * layer + 3] for layer in range(LAYERS)]

    def turn(xs):
        block = channels // devices
        uses = [(0, 0), (0, 1), (1, 1), (1, 2), (2, 2)]

        def body(scalars, *refs):
            row = lax.broadcasted_iota(jnp.int32, (channels, 1), 0)
            index = row // block
            lanes = lax.broadcasted_iota(jnp.int32, (channels, channels), 1)
            picks = []
            for layer in range(LAYERS):
                target = jnp.zeros_like(row)
                for place, bit in enumerate(b for g in groups[layer] for b in g):
                    target = target | (((index >> (width - 1 - place)) & 1) << bit)
                source = (target ^ scalars[LAYERS]) * block + row % block
                picks.append(jnp.where(lanes == source, 1.0, 0.0))
            for n, (x, order) in enumerate(uses):
                refs[LAYERS + n][...] = dot_nt(picks[order], refs[x][...])

        return dict(zip(uses, line(body, xs, [(channels, bins)] * len(uses))))

    def center(g, gu, w, carried=None):
        carry = [] if carried is None else [carried]

        def body(_, g_ref, gu_ref, w_ref, *refs):
            refs[len(carry)][...] = g_ref[...] + dot_nt(gu_ref[...], w_ref[...])
            if carry:
                refs[2][...] = refs[0][...]

        return line(body, [g, gu, w, *carry], [g.shape] + [c.shape for c in carry])

    def advance(base, sides, wp, wq, pull=None, slope=None, work=0):
        def body(_, base_ref, p_ref, q_ref, wp_ref, wq_ref, *refs):
            g = base_ref[...] + dot_nt(p_ref[...], wp_ref[...])
            g = g + dot_nt(q_ref[...], wq_ref[...])
            if pull is None:
                refs[0][...] = g
            else:
                pull_ref, slope_ref, g_ref, gu_ref = refs
                g = g + pull_ref[...]
                g_ref[...] = g
                gu_ref[...] = g * slope_ref[...]

        ins = [base, *sides, wp, wq]
        if pull is None:
            return line(body, ins, [base.shape], work=work)
        return line(body, ins + [pull, slope], [base.shape] * 2, work=work)

    rows = channels // 2

    def add(layer, x, body, inputs, taps, work):
        keep, send = line(body, [x, *inputs], [(rows, len(taps) * channels)] * 2, work=work)
        sums[layer].add(send, keep)
        columns[layer].extend(taps)

    def store(outs, place, value):
        for n, out_ref in enumerate(outs):
            out_ref[:, place] = value[rows * n : rows * (n + 1), :]

    def middle(layer, work):
        def body(_, x_ref, a_ref, b_ref, *outs):
            both = jnp.concatenate([a_ref[...], b_ref[...]], axis=0)
            store(outs, slice(0, channels), dot(x_ref[...], both))

        add(layer, xt[layer, layer], body, [gu["a", layer], gu["b", layer]], [(layer, 1)], work)

    def terms(layer, work):
        below = layer - 1
        ins = [*halos["a", layer], *halos["b", layer]]
        if layer:
            ins += [gu["a", below], gu["b", below], xt[below, layer]]

        def body(s_ref, x_ref, *refs):
            outs = refs[len(ins) :]
            for k in range(2):
                column = s_ref[layer] if k == 0 else 1 - s_ref[layer]
                place = pl.ds(pl.multiple_of(column * channels, channels), channels)
                both = jnp.concatenate([refs[k][...], refs[2 + k][...]], axis=0)
                store(outs, place, dot(x_ref[...], both))
            if layer:
                both = jnp.concatenate([refs[4][...], refs[5][...]], axis=0)
                store(outs, slice(2 * channels, 3 * channels), dot(refs[6][...], both))

        taps = [(layer, 0), (layer, 2)] + ([(below, 1)] if layer else [])
        add(layer, xt[layer, layer], body, ins, taps, work)

    sums = [Scatter(line, groups[layer]) for layer in range(LAYERS)]
    columns = [[] for _ in range(LAYERS)]
    w, base, g, gu, halos = {}, {}, {}, {}, {}
    pull, slope = {}, {}
    for name, work in ORDER:
        kind, layer = name[:-1], int(name[-1]) if name[-1].isdigit() else None
        if name == "top":
            g["a"], gu["a", 2] = top()
            halos["a", 2] = halo(gu["a", 2], 2)
        elif name == "prep":
            x1, x2, *pairs, g["b"], carried = prepare()
            gu["b", 2] = carried
            for c, key in enumerate("ab"):
                h = pairs[4 * c : 4 * c + 4]
                pull[key, 1], slope[key, 1], pull[key, 2], slope[key, 2] = h
        elif name == "turn":
            xt = turn((features, x1, x2))
        elif name == "w":
            w = weights()
        elif name == "ca2":
            base["a"], gu["b", 2] = center(g["a"], gu["a", 2], w[2][1], carried)
            halos["b", 2] = halo(gu["b", 2], 2)
        elif kind in ("ca", "cb"):
            key = kind[1]
            (base[key],) = center(g[key], gu[key, layer], w[layer][1])
        elif kind in ("aa", "ab"):
            key = kind[1]
            args = base[key], halos[key, layer], w[layer][0], w[layer][2]
            if layer:
                g[key], gu[key, layer - 1] = advance(
                    *args, pull[key, layer], slope[key, layer], work=work
                )
                halos[key, layer - 1] = halo(gu[key, layer - 1], layer - 1)
            else:
                (g[key],) = advance(*args, work=work)
        elif kind == "m":
            middle(layer, work)
        elif kind == "t":
            terms(layer, work)
        elif sums[layer].groups:
            sums[layer].step(work)
    for s in sums:
        while s.groups:
            s.step(0)
    done = [s.result() for s in sums]
    taps = {}
    for total, names in zip(done, columns):
        for n, tap in enumerate(names):
            taps[tap] = total[:, n * channels : (n + 1) * channels]
    grads = jnp.stack([jnp.stack([taps[layer, k] for k in range(3)]) for layer in range(LAYERS)])
    grads = grads * scale
    return jnp.concatenate([g["a"], g["b"]], axis=0), grads


def solution(mesh):
    in_specs = (P("seq", None), P(None, "seq", None), P(None, "seq", None), P("seq", None), P())
    out_specs = (P("seq", None), P(None, None, "seq", None))
    return jax.shard_map(shards, mesh=mesh, in_specs=in_specs, out_specs=out_specs, check_vma=False)
```
